256 devices in a mesh: head: 4 (over y_lo, core), inner: 16 (over y_hi, z), outer: 4 (over x).
Axes of the slice: x: 4, y: 4 (y_hi: 2, y_lo: 2; y = y_hi * 2 + y_lo), z: 8, core: 2. Of those that a mesh axis runs over, the one named last changes fastest.
Arguments:
- queries: bfloat16 [8192, 3072], P(('head', 'inner', 'outer')), may hold values from -8 to 8
- keys: bfloat16 [8192, 512], P(('head', 'inner', 'outer')), may hold values from -6 to 6
- values: bfloat16 [8192, 512], P(('head', 'inner', 'outer')), may hold values from -6 to 6
- outputs: bfloat16 [8192, 3072], P(('head', 'inner', 'outer')), may hold values from -6 to 6
- log_norms: bfloat16 [8192, 24], P(('head', 'inner', 'outer')), as said below
- grad_output: bfloat16 [8192, 6144], P(('head', 'inner', 'outer')), may hold values from -6 to 6
- w_output: bfloat16 [3072, 6144], P('head', 'inner'), may hold values from -0.078125 to 0.078125
- block_order: int32 [256], replicated, may hold values from 0 to 255, as said below
Outputs:
- grad_query: bfloat16 [8192, 3072], P(('head', 'inner', 'outer'))
- grad_key: bfloat16 [8192, 512], P(('head', 'inner', 'outer'))
- grad_value: bfloat16 [8192, 512], P(('head', 'inner', 'outer'))
The draws below stay inside these ranges and needn't reach their ends.
Inputs may be any that keep to these rules, and one draw needn't show every extreme that they name: `block_order`: a permutation of the 256 sequence blocks. `log_norms`: drawn as log(p + 1) + 1.1 + 0.5 u, where p is the row's sequence position and u is uniform in [0, 1); it stands in for a stored log-sum-exp and is not recomputed from queries and keys.
All inputs are finite; a program needn't handle non-finite values.
Results may differ from the reference program's by a relative error of at most 0.018.
Values may be sent and summed in bfloat16 or wider, within the bound.
No kernel may reach another device: no remote copies, remote signals or barrier semaphores. Data moves between devices by JAX's collectives and lax.ppermute only.
A program may use at most 128 MiB of HBM per device.

```python
import jax
import jax.numpy as jnp
from jax import lax

D = 6144
HD = 128
QH = 24
KH = 4
TOK_DEV = 32
BLOCKS = 256
TOKENS = 8192


def block_table(key):
    return jax.random.permutation(key, BLOCKS).astype(jnp.int32)


def draw_block_order(key, part):
    return block_table(key)


def draw_log_norms(key, part):
    order_table = block_table(key)
    key = jax.random.fold_in(key, 7)
    row_ids = jnp.arange(TOKENS, dtype=jnp.int32)
    position = order_table[row_ids // TOK_DEV] * TOK_DEV + row_ids % TOK_DEV
    jitter = jax.random.uniform(key, (TOKENS, QH), jnp.float32)
    log_count = jnp.log(position.astype(jnp.float32) + 1.0)[:, None]
    return (log_count + 1.1 + 0.5 * jitter).astype(jnp.bfloat16)


def shard_levels(own_key, shape, cuts, least, largest):
    loudness = 1.0
    for axis_at, parts in cuts:
        steps = jax.random.uniform(jax.random.fold_in(jax.random.fold_in(own_key, 6), axis_at), (parts,), jnp.float32, least / len(cuts), largest / len(cuts))
        loudness = loudness * jnp.repeat(jnp.exp(steps), shape[axis_at] // parts).reshape((-1,) + (1,) * (len(shape) - 1 - axis_at))
    return loudness


def gaussian(rng, shape, width, limit, cuts=(), kind=jnp.bfloat16):
    entries = width * jax.random.normal(rng, shape, jnp.float32)
    if cuts:
        entries = entries * shard_levels(rng, shape, cuts, -0.22, 0.18)
    return jnp.clip(entries, -limit, limit).astype(kind)


def setup_inputs(seed: int = 0) -> dict:
    seeds = jax.random.split(jax.random.key(seed), 9)
    queries = gaussian(seeds[0], (TOKENS, QH * HD), 1.5, 8.0, ((0, 256),))
    keys = gaussian(seeds[1], (TOKENS, KH * HD), 1.0, 6.0, ((0, 256),))
    values = gaussian(seeds[2], (TOKENS, KH * HD), 1.0, 6.0, ((0, 256),))
    outputs = gaussian(seeds[3], (TOKENS, QH * HD), 1.0, 6.0, ((0, 256),))
    log_norms = draw_log_norms(jax.random.fold_in(seeds[8], 71), 0)
    grad_output = gaussian(seeds[5], (TOKENS, D), 1.0, 6.0, ((0, 256),))
    w_output = gaussian(seeds[6], (QH * HD, D), D ** -0.5, 0.078125, ((0, 4), (1, 16)))
    block_order = draw_block_order(jax.random.fold_in(seeds[8], 71), 0)
    return {"queries": queries, "keys": keys, "values": values, "outputs": outputs, "log_norms": log_norms, "grad_output": grad_output, "w_output": w_output, "block_order": block_order}


def reference(queries, keys, values, outputs, log_norms, grad_output, w_output, block_order):
    grad_attn = jnp.dot(grad_output, w_output.T, preferred_element_type=jnp.float32).astype(jnp.bfloat16)
    row_ids = jnp.arange(TOKENS, dtype=jnp.int32)
    position = block_order[row_ids // TOK_DEV] * TOK_DEV + row_ids % TOK_DEV
    visible = position[:, None] >= position[None, :]
    score_scale = HD ** -0.5
    group_size = QH // KH

    def one_head(head_id):
        kv_id = head_id // group_size
        query_h = lax.dynamic_slice_in_dim(queries, head_id * HD, HD, 1)
        output_h = lax.dynamic_slice_in_dim(outputs, head_id * HD, HD, 1)
        dattn_h = lax.dynamic_slice_in_dim(grad_attn, head_id * HD, HD, 1)
        key_g = lax.dynamic_slice_in_dim(keys, kv_id * HD, HD, 1)
        value_g = lax.dynamic_slice_in_dim(values, kv_id * HD, HD, 1)
        norm_h = lax.dynamic_slice_in_dim(log_norms, head_id, 1, 1)[:, 0].astype(jnp.float32)
        scores = jnp.dot(query_h, key_g.T, preferred_element_type=jnp.float32) * score_scale
        probs = jnp.where(visible, jnp.exp(scores - norm_h[:, None]), jnp.float32(0.0))
        probs_low = probs.astype(jnp.bfloat16)
        grad_v = jnp.dot(probs_low.T, dattn_h, preferred_element_type=jnp.float32)
        grad_probs = jnp.dot(dattn_h, value_g.T, preferred_element_type=jnp.float32)
        delta = jnp.sum(dattn_h.astype(jnp.float32) * output_h.astype(jnp.float32), axis=1)
        grad_scores = (probs * (grad_probs - delta[:, None])).astype(jnp.bfloat16)
        grad_q = jnp.dot(grad_scores, key_g, preferred_element_type=jnp.float32) * score_scale
        grad_k = jnp.dot(grad_scores.T, query_h, preferred_element_type=jnp.float32) * score_scale
        return grad_q, grad_k, grad_v

    head_ids = jnp.arange(QH, dtype=jnp.int32)
    all_q, all_k, all_v = lax.map(one_head, head_ids)
    grad_query = all_q.transpose(1, 0, 2).reshape(TOKENS, QH * HD).astype(jnp.bfloat16)
    grad_key = all_k.reshape(KH, group_size, TOKENS, HD).sum(axis=1)
    grad_key = grad_key.transpose(1, 0, 2).reshape(TOKENS, KH * HD).astype(jnp.bfloat16)
    grad_value = all_v.reshape(KH, group_size, TOKENS, HD).sum(axis=1)
    grad_value = grad_value.transpose(1, 0, 2).reshape(TOKENS, KH * HD).astype(jnp.bfloat16)
    return (grad_query, grad_key, grad_value)
```

```python
import jax
import jax.numpy as jnp
from jax import lax
from jax.experimental import pallas as pl
from jax.experimental.pallas import tpu as pltpu
from jax.sharding import PartitionSpec as P

HD = 128
LANES = 128
BF = jnp.bfloat16
F32 = jnp.float32
HIDE = -1e30
SCALE = HD ** (-0.5)
LOG2E = 1.4426950408889634
ID_LANE = 32
CHUNK = 256
VMEM_BYTES = 48 * 1024 * 1024


def call(kernel, out_shape, **options):
    return pl.pallas_call(
        kernel,
        out_shape=out_shape,
        compiler_params=pltpu.CompilerParams(vmem_limit_bytes=VMEM_BYTES),
        **options,
    )


def xor_route(axis, mask):
    return [(i, i ^ mask) for i in range(lax.axis_size(axis))]


def split_three(x):
    high = x.astype(BF)
    rest = x - high.astype(F32)
    mid = rest.astype(BF)
    low = (rest - mid.astype(F32)).astype(BF)
    return high, mid, low


def pick_three(x, lane_rest):
    high, mid, low = split_three(x)
    zero = jnp.zeros_like(x)
    return (
        jnp.where(lane_rest == 0, high.astype(F32), zero)
        + jnp.where(lane_rest == 1, mid.astype(F32), zero)
        + jnp.where(lane_rest == 2, low.astype(F32), zero)
    ).astype(BF)


def lane_head(shape):
    lane = lax.broadcasted_iota(jnp.int32, shape, len(shape) - 1)
    head = lax.shift_right_logical(lane * 171, 9)
    return lane, head, lane - 3 * head


def pack_tokens_kernel(q_ref, o_ref, k_ref, v_ref, n_ref, out_ref):
    head_groups, rows, _ = out_ref.shape
    group = n_ref.shape[1] // head_groups
    width = group * HD
    norms = n_ref[...].astype(F32)
    _, lane_h, lane_rest = lane_head((rows, LANES))
    for h in range(head_groups):
        out_ref[h, :, :width] = q_ref[:, h * width : (h + 1) * width]
        spread = jnp.zeros((rows, LANES), F32)
        for j in range(group):
            column = norms[:, h * group + j : h * group + j + 1] * (-(HD**0.5))
            spread = jnp.where(lane_h == j, column, spread)
        out_ref[h, :, width : width + LANES] = pick_three(spread, lane_rest)
        at = width + LANES
        out_ref[h, :, at : at + HD] = k_ref[:, h * HD : (h + 1) * HD]
        out_ref[h, :, at + HD : at + 2 * HD] = v_ref[:, h * HD : (h + 1) * HD]
        at += 2 * HD
        out_ref[h, :, at : at + width] = o_ref[:, h * width : (h + 1) * width]


def pack_grads_kernel(place_ref, g_ref, out_ref):
    high_bit, low_bit = place_ref[0], place_ref[1]
    groups, _, wide = out_ref.shape
    width = wide // 4
    for zg in range(groups):
        for rel in range(4):
            block = (
                jnp.bitwise_xor(high_bit, rel // 2) * (2 * groups)
                + 2 * zg
                + jnp.bitwise_xor(low_bit, rel % 2)
            )
            start = pl.multiple_of(block * width, LANES)
            out_ref[zg, :, rel * width : (rel + 1) * width] = g_ref[:, pl.ds(start, width)]


def project_kernel(place_ref, ga, gb, gc, w0, w1, w2, w3, out_ref):
    my_head = place_ref[2]
    groups, rows, wide = ga.shape
    width = wide // 4
    weights = (w0, w1, w2, w3)
    parts = ((ga, 0, 0), (gb, 0, 2), (gc, 0, 1), (gc, groups, 3))
    for ref, at, mask in parts:
        tokens = ref[at : at + groups].reshape(groups * rows, wide)
        total = jnp.zeros((groups * rows, w0.shape[0]), F32)
        for j, w_ref in enumerate(weights):
            total += lax.dot_general(
                tokens[:, j * width : (j + 1) * width],
                w_ref[...],
                (((1,), (1,)), ((), ())),
                preferred_element_type=F32,
            )
        owner = jnp.bitwise_xor(my_head, mask)
        out_ref[:, owner] = total.astype(BF).reshape(groups, rows, -1)


def centre_kernel(p_ref, o_ref, out_ref):
    total = p_ref[0].astype(F32)
    for part in range(1, p_ref.shape[0]):
        total += p_ref[part].astype(F32)
    grads = total.astype(BF)
    rows, width = grads.shape
    out_ref[:, :width] = grads
    product = grads.astype(F32) * o_ref[...].astype(F32)
    _, lane_h, lane_rest = lane_head((rows, LANES))
    spread = jnp.zeros((rows, LANES), F32)
    for j in range(width // HD):
        delta = jnp.sum(product[:, j * HD : (j + 1) * HD], axis=1, keepdims=True)
        spread = jnp.where(lane_h == j, -delta, spread)
    out_ref[:, width:] = pick_three(spread, lane_rest)


def attend_kernel(
    place_ref, qid_ref, kid_ref, q0, q1, q2, q3, d0, d1, d2, d3, kv_ref,
    dq_ref, dkv_ref, q_all, d_all, dq_acc,
):
    step = pl.program_id(0)
    my_inner, my_outer = place_ref[3], place_ref[4]
    part_rows = q0.shape[0]
    rows = 4 * part_rows
    width = q0.shape[1] - LANES
    group = width // HD
    tok = dq_ref.shape[2]

    @pl.when(step == 0)
    def _():
        for part, (q_part, d_part) in enumerate(zip((q0, q1, q2, q3), (d0, d1, d2, d3))):
            at = slice(part * part_rows, (part + 1) * part_rows)
            q_all[at, :width] = q_part[:, :width]
            hidden = jnp.where(kid_ref[...] > qid_ref[at, :], F32(HIDE), F32(0.0))
            q_all[at, width:] = (q_part[:, width:].astype(F32) + hidden).astype(BF)
            d_all[at, :] = d_part[...]
        dq_acc[...] = jnp.zeros_like(dq_acc)

    chunk = kv_ref.shape[0] * kv_ref.shape[1]
    kv = kv_ref[...].reshape(chunk, 2 * HD)
    keys, values = kv[:, :HD], kv[:, HD:]
    lane = lax.broadcasted_iota(jnp.int32, (chunk, LANES), 1)
    block = step * (chunk // tok) + lax.broadcasted_iota(jnp.int32, (chunk, LANES), 0) // tok
    one_hot = jnp.where(lane == ID_LANE + block, F32(1.0), F32(0.0))
    per_step = kv_ref.shape[0]
    diagonal = my_inner // per_step == step

    def run(masked):
        dk = jnp.zeros((chunk, HD), F32)
        dv = jnp.zeros((chunk, HD), F32)
        if masked:
            r = lax.broadcasted_iota(jnp.int32, (chunk, rows), 0)
            c = lax.broadcasted_iota(jnp.int32, (chunk, rows), 1)
            shift = (my_inner % per_step) * (part_rows // tok)
            future = (r // tok - shift == c // tok) & (r % tok > c % tok) & (c < part_rows)
        for j in range(group):
            mine = (lane >= 3 * j) & (lane < 3 * j + 3)
            pick = jnp.where(mine, F32(1.0), F32(0.0))
            keys_wide = jnp.concatenate([keys, (pick + one_hot).astype(BF)], axis=1)
            values_wide = jnp.concatenate([values, pick.astype(BF)], axis=1)
            at = slice(j * HD, (j + 1) * HD)
            q_j, d_j = q_all[:, at], d_all[:, at]
            q_wide = jnp.concatenate([q_j, q_all[:, width:]], axis=1)
            d_wide = jnp.concatenate([d_j, d_all[:, width:]], axis=1)
            contract = (((1,), (1,)), ((), ()))
            scores = lax.dot_general(keys_wide, q_wide, contract, preferred_element_type=F32)
            grad_probs = lax.dot_general(values_wide, d_wide, contract, preferred_element_type=F32)
            probs = jnp.exp2(scores * F32(SCALE * LOG2E))
            if masked:
                probs = jnp.where(future, F32(0.0), probs)
            grad_scores = (probs * grad_probs).astype(BF)
            dv += jnp.dot(probs.astype(BF), d_j, preferred_element_type=F32)
            dk += jnp.dot(grad_scores, q_j, preferred_element_type=F32)
            dq_acc[at, :] += lax.dot_general(
                keys, grad_scores, (((0,), (0,)), ((), ())), preferred_element_type=F32
            )
        dk = (dk * F32(SCALE)).astype(BF)
        dv = dv.astype(BF)
        heads = part_rows // tok
        for i in range(per_step):
            for h in range(heads):
                at = slice((i * heads + h) * tok, (i * heads + h + 1) * tok)
                dkv_ref[h, i, :, :HD] = dk[at]
                dkv_ref[h, i, :, HD:] = dv[at]

    pl.when(diagonal)(lambda: run(True))
    pl.when(jnp.logical_not(diagonal))(lambda: run(False))

    @pl.when(step == pl.num_programs(0) - 1)
    def _():
        for j in range(group):
            at = slice(j * HD, (j + 1) * HD)
            grads = (dq_acc[at, :].T * F32(SCALE)).astype(BF)
            for part in range(4):
                owner = lax.rem(my_outer + 4 - part, 4)
                for h in range(part_rows // tok):
                    start = part * part_rows + h * tok
                    dq_ref[h, owner, :, at] = grads[start : start + tok]


def finish_kernel(dq_ref, dkv_ref, gq_ref, gk_ref, gv_ref):
    heads, parts, _, width = dq_ref.shape
    for h in range(heads):
        total = dq_ref[h, 0].astype(F32)
        for p in range(1, parts):
            total += dq_ref[h, p].astype(F32)
        gq_ref[:, h * width : (h + 1) * width] = total.astype(BF)
        total = dkv_ref[h, 0].astype(F32)
        for p in range(1, dkv_ref.shape[1]):
            total += dkv_ref[h, p].astype(F32)
        total = total.astype(BF)
        gk_ref[:, h * HD : (h + 1) * HD] = total[:, :HD]
        gv_ref[:, h * HD : (h + 1) * HD] = total[:, HD:]


def shape_of(*dims, dtype=BF):
    return jax.ShapeDtypeStruct(dims, dtype)


def body(queries, keys, values, outputs, log_norms, grad_output, w_output, block_order):
    tok = grad_output.shape[0]
    heads = lax.axis_size("head")
    inners = lax.axis_size("inner")
    outers = lax.axis_size("outer")
    head, inner, outer = (lax.axis_index(a) for a in ("head", "inner", "outer"))
    z_count = inners // 2
    z_groups = z_count // 2
    width = queries.shape[1] // heads
    k_width = w_output.shape[1]
    part_rows = heads * tok
    place = jnp.stack([inner // z_count, inner % 2, head, inner, outer]).astype(jnp.int32)
    smem = pl.BlockSpec(memory_space=pltpu.SMEM)
    vmem = pl.BlockSpec(memory_space=pltpu.VMEM)

    weights = [w_output] + [
        lax.ppermute(w_output, "inner", xor_route("inner", m))
        for m in (1, z_count, z_count + 1)
    ]
    grads_out = call(
        pack_grads_kernel,
        shape_of(z_groups, tok, 4 * k_width),
        in_specs=[smem, vmem],
        out_specs=vmem,
    )(place, grad_output)
    strides = [
        [y * z_count + p + 2 * g for g in range(z_groups)] for y in range(2) for p in range(2)
    ]
    grads_a = lax.all_to_all(
        grads_out, "inner", split_axis=0, concat_axis=0, axis_index_groups=strides, tiled=True
    )

    packed = call(
        pack_tokens_kernel,
        shape_of(heads, tok, 2 * width + LANES + 2 * HD),
        in_specs=[vmem] * 5,
        out_specs=vmem,
    )(queries, outputs, keys, values, log_norms)
    mine = lax.all_to_all(packed, "head", split_axis=0, concat_axis=0, tiled=True)
    mine = mine.reshape(part_rows, -1)
    q_part = mine[:, : width + LANES]
    kv_part = mine[:, width + LANES : width + LANES + 2 * HD]
    o_part = mine[:, width + LANES + 2 * HD :]

    grads_b = lax.ppermute(grads_a, "head", xor_route("head", 2))
    grads_c = lax.ppermute(
        jnp.concatenate([grads_a, grads_b], 0), "head", xor_route("head", 1)
    )
    partial = call(
        project_kernel,
        shape_of(z_groups, heads, tok, width),
        in_specs=[smem] + [vmem] * 7,
        out_specs=vmem,
    )(place, grads_a, grads_b, grads_c, *weights)
    partial = lax.all_to_all(
        partial, "inner", split_axis=0, concat_axis=0, axis_index_groups=strides, tiled=True
    )
    d_part = call(
        centre_kernel,
        shape_of(part_rows, width + LANES),
        in_specs=[vmem] * 2,
        out_specs=vmem,
    )(partial.reshape(z_groups, part_rows, width), o_part)

    def around(x):
        return [x] + [
            lax.ppermute(x, "outer", [(i, (i + d) % outers) for i in range(outers)])
            for d in range(1, outers)
        ]

    q_parts = around(q_part)
    kv_all = lax.all_to_all(
        jnp.broadcast_to(kv_part[None], (inners,) + kv_part.shape),
        "inner", split_axis=0, concat_axis=0, tiled=True,
    )
    d_parts = around(d_part)

    order = block_order.reshape(heads, inners, outers)
    k_ids = lax.dynamic_index_in_dim(order, outer, 2, keepdims=False).T.reshape(-1)
    q_ids = lax.dynamic_index_in_dim(order, inner, 1, keepdims=False).T
    q_ids = jnp.concatenate(
        [lax.dynamic_index_in_dim(q_ids, (outer - d) % outers, 0) for d in range(outers)], 0
    ).reshape(-1)
    kid_row = jnp.full((1, LANES), -1.0, F32)
    kid_row = lax.dynamic_update_slice(kid_row, k_ids.astype(F32)[None], (0, ID_LANE))
    qid_col = jnp.repeat(q_ids.astype(F32), tok)[:, None]

    per_step = CHUNK // part_rows
    rows = outers * part_rows
    whole = lambda *shape: pl.BlockSpec(shape, lambda c: (0,) * len(shape))
    dq_out, dkv_out = call(
        attend_kernel,
        (
            shape_of(heads, outers, tok, width),
            shape_of(heads, inners, tok, 2 * HD),
        ),
        grid=(inners // per_step,),
        in_specs=[smem, whole(rows, 1), whole(1, LANES)]
        + [whole(part_rows, width + LANES)] * 8
        + [pl.BlockSpec((per_step, part_rows, 2 * HD), lambda c: (c, 0, 0))],
        out_specs=(
            whole(heads, outers, tok, width),
            pl.BlockSpec((heads, per_step, tok, 2 * HD), lambda c: (0, c, 0, 0)),
        ),
        scratch_shapes=[
            pltpu.VMEM((rows, width + LANES), BF),
            pltpu.VMEM((rows, width + LANES), BF),
            pltpu.VMEM((width, rows), F32),
        ],
    )(place, qid_col, kid_row, *q_parts, *d_parts, kv_all)

    dq_back = lax.all_to_all(
        dq_out.reshape(heads * outers, tok, width),
        ("head", "outer"), split_axis=0, concat_axis=0, tiled=True,
    ).reshape(heads, outers, tok, width)
    dkv_back = lax.all_to_all(
        dkv_out.reshape(heads * inners, tok, 2 * HD),
        ("head", "inner"), split_axis=0, concat_axis=0, tiled=True,
    ).reshape(heads, inners, tok, 2 * HD)
    return call(
        finish_kernel,
        (
            shape_of(tok, heads * width),
            shape_of(tok, heads * HD),
            shape_of(tok, heads * HD),
        ),
        in_specs=[vmem] * 2,
        out_specs=(vmem,) * 3,
    )(dq_back, dkv_back)


def solution(mesh):
    tokens = P(("head", "inner", "outer"), None)
    in_specs = (tokens,) * 6 + (P("head", "inner"), P())
    return jax.shard_map(
        body, mesh=mesh, in_specs=in_specs, out_specs=(tokens,) * 3, check_vma=False
    )
```

```python
import functools

import jax
import jax.numpy as jnp
from jax import lax
from jax.experimental import pallas as pl
from jax.experimental.pallas import tpu as pltpu
from jax.sharding import PartitionSpec as P

HD = 128
LANES = 128
BF = jnp.bfloat16
F32 = jnp.float32
HIDE = -1e30
SCALE = HD ** (-0.5)
LOG2E = 1.4426950408889634
ID_LANE = 32
CHUNK = 256
VMEM_BYTES = 28 * 1024 * 1024
WEIGHT_MASKS = (0, 2, 4, 6)
TOKEN_MASKS = (0, 1, 8, 9)
OFFSETS = (-1, 0, 1, 2, 3, 4, -3, -2)
NEXT = 4


def call(kernel, out_shape, **options):
    return pl.pallas_call(
        kernel,
        out_shape=out_shape,
        compiler_params=pltpu.CompilerParams(vmem_limit_bytes=VMEM_BYTES),
        **options,
    )


def xor_route(axis, mask):
    return [(i, i ^ mask) for i in range(lax.axis_size(axis))]


def split_three(x):
    high = x.astype(BF)
    rest = x - high.astype(F32)
    mid = rest.astype(BF)
    low = (rest - mid.astype(F32)).astype(BF)
    return high, mid, low


def pick_three(x, lane_rest):
    high, mid, low = split_three(x)
    zero = jnp.zeros_like(x)
    return (
        jnp.where(lane_rest == 0, high.astype(F32), zero)
        + jnp.where(lane_rest == 1, mid.astype(F32), zero)
        + jnp.where(lane_rest == 2, low.astype(F32), zero)
    ).astype(BF)


def lane_head(shape):
    lane = lax.broadcasted_iota(jnp.int32, shape, len(shape) - 1)
    head = lax.shift_right_logical(lane * 171, 9)
    return lane, head, lane - 3 * head


def ids_kernel(place_ref, order_ref, qid_ref, near_ref, far_ref):
    inner, outer, my_z = place_ref[0], place_ref[2], place_ref[3]
    zs, outers, heads = len(OFFSETS), 4, 4
    inners = 2 * zs
    tok = qid_ref.shape[0] // (outers * heads)
    for d in range(outers):
        o = jnp.bitwise_xor(outer, d)
        for h in range(heads):
            block = order_ref[(h * inners + inner) * outers + o]
            at = (d * heads + h) * tok
            qid_ref[at : at + tok, :] = jnp.full((tok, 1), block, jnp.int32).astype(F32)
    lane = lax.broadcasted_iota(jnp.int32, (1, LANES), 1)
    plane = inner // zs
    for ref, y in ((near_ref, plane), (far_ref, 1 - plane)):
        ids = jnp.full((1, LANES), -1, jnp.int32)
        for n, offset in enumerate(OFFSETS):
            z = lax.rem(my_z + zs + offset, zs)
            for h in range(heads):
                block = order_ref[(h * inners + y * zs + z) * outers + outer]
                ids = jnp.where(lane == ID_LANE + n * heads + h, block, ids)
        ref[...] = ids.astype(F32)


def pack_tokens_kernel(place_ref, q_ref, o_ref, k_ref, v_ref, n_ref, *out_refs):
    my_head = place_ref[1]
    rows = q_ref.shape[0]
    heads = len(out_refs)
    width = q_ref.shape[1] // heads
    group = width // HD
    norms = n_ref[...].astype(F32)
    _, _, lane_rest = lane_head((rows, LANES))
    lane, lane_h, _ = lane_head((heads * group, LANES))
    row = lax.broadcasted_iota(jnp.int32, (heads * group, LANES), 0)
    for r, out_ref in enumerate(out_refs):
        h = jnp.bitwise_xor(my_head, r)
        columns = pl.ds(pl.multiple_of(h * width, LANES), width)
        narrow = pl.ds(pl.multiple_of(h * HD, LANES), HD)
        out_ref[:, :width] = q_ref[:, columns]
        chosen = (row == h * group + lane_h) & (lane_h < group)
        spread = lax.dot_general(
            norms,
            jnp.where(chosen, F32(1.0), F32(0.0)),
            (((0,), (0,)), ((), ())),
            preferred_element_type=F32,
        ) * F32(-(HD**0.5))
        out_ref[:, width : width + LANES] = pick_three(spread, lane_rest)
        at = width + LANES
        out_ref[:, at : at + HD] = k_ref[:, narrow]
        out_ref[:, at + HD : at + 2 * HD] = v_ref[:, narrow]
        out_ref[:, at + 2 * HD :] = o_ref[:, columns]


def unpack_tokens_kernel(place_ref, t0, t1, t2, t3, q_ref, kv_ref, o_ref, kv_here, sems):
    my_head = place_ref[1]
    rows = t0.shape[0]
    q_width, kv_width = q_ref.shape[1], kv_here.shape[1]
    for r, ref in enumerate((t0, t1, t2, t3)):
        h = jnp.bitwise_xor(my_head, r)
        at = pl.ds(pl.multiple_of(h * rows, rows), rows)
        q_ref[at, :] = ref[:, :q_width]
        kv_here[at, :] = ref[:, q_width : q_width + kv_width]
        o_ref[at, :] = ref[:, q_width + kv_width :]
    for copy in copy_in([(kv_here, kv_ref.at[n]) for n in range(kv_ref.shape[0])], sems):
        copy.wait()


def pack_grads_kernel(place_ref, g_ref, *out_refs):
    my_inner = place_ref[0]
    width = out_refs[0].shape[1] // len(WEIGHT_MASKS)
    for m, out_ref in enumerate(out_refs):
        for r, mask in enumerate(WEIGHT_MASKS):
            block = jnp.bitwise_xor(my_inner, TOKEN_MASKS[m] ^ mask)
            start = pl.multiple_of(block * width, LANES)
            out_ref[:, r * width : (r + 1) * width] = g_ref[:, pl.ds(start, width)]


def copy_in(pairs, sems):
    copies = [pltpu.make_async_copy(a, b, sems.at[n]) for n, (a, b) in enumerate(pairs)]
    for copy in copies:
        copy.start()
    return copies


def pack_kernel(
    place_ref, order_ref, w_ref, g_ref, q_ref, o_ref, k_ref, v_ref, n_ref,
    wq_ref, s0, s1, s2, s3, t0, t1, t2, t3, qid_ref, near_ref, far_ref,
    g_here, q_here, o_here, k_here, v_here, n_here, sems,
):
    quarter = wq_ref.shape[0]
    rows = pl.ds(pl.multiple_of(place_ref[2] * quarter, 16), quarter)
    pairs = (
        (w_ref.at[rows], wq_ref), (g_ref, g_here), (q_ref, q_here), (o_ref, o_here),
        (k_ref, k_here), (v_ref, v_here), (n_ref, n_here),
    )
    copies = copy_in(pairs, sems)
    ids_kernel(place_ref, order_ref, qid_ref, near_ref, far_ref)
    for copy in copies:
        copy.wait()
    pack_grads_kernel(place_ref, g_here, s0, s1, s2, s3)
    pack_tokens_kernel(place_ref, q_here, o_here, k_here, v_here, n_here, t0, t1, t2, t3)


def project_kernel(place_ref, ga, gb, gc, gd, w0, x0, x1, x2, x3, *refs):
    out_refs, (g_all, w_all, sems) = refs[:-3], refs[-3:]
    my_head, my_outer = place_ref[1], place_ref[2]
    groups, rows, wide = ga.shape
    width = w0.shape[1]
    count = groups * rows
    quarter = x0.shape[1]
    pairs = [(ref, g_all.at[n]) for n, ref in enumerate((ga, gb, gc, gd))]
    pairs.append((w0, w_all.at[:, pl.ds(0, width)]))
    for d, ref in enumerate((x0, x1, x2, x3)):
        owner = lax.rem(my_outer + 4 - d, 4)
        at = pl.ds(pl.multiple_of(owner * quarter, 16), quarter)
        for j in range(ref.shape[0]):
            pairs.append((ref.at[j], w_all.at[at, pl.ds((1 + j) * width, width)]))
    for copy in copy_in(pairs, sems):
        copy.wait()
    total = lax.dot_general(
        g_all[...].reshape(4 * count, wide), w_all[...], (((1,), (1,)), ((), ())),
        preferred_element_type=F32,
    ).astype(BF)
    for n, mask in enumerate((0, 2, 1, 3)):
        owner = jnp.bitwise_xor(my_head, mask)
        for m, out_ref in enumerate(out_refs):
            at = n * count + m * rows
            out_ref[owner] = total[at : at + rows]


def centre_kernel(place_ref, o_ref, p0, p1, p2, p3, out_ref):
    total = p0[...].astype(F32)
    for p_ref in (p1, p2, p3):
        total += p_ref[...].astype(F32)
    rows, width = o_ref.shape
    grads = total.astype(BF).reshape(rows, width)
    out_ref[:, :width] = grads
    product = grads.astype(F32) * o_ref[...].astype(F32)
    _, lane_h, lane_rest = lane_head((rows, LANES))
    spread = jnp.zeros((rows, LANES), F32)
    for j in range(width // HD):
        delta = jnp.sum(product[:, j * HD : (j + 1) * HD], axis=1, keepdims=True)
        spread = jnp.where(lane_h == j, -delta, spread)
    out_ref[:, width:] = pick_three(spread, lane_rest)


def attend(
    place_ref, qid_ref, kid_ref, kv_ref, write, q_all, d_all, dq_acc, tok, spans, diagonal
):
    rows = q_all.shape[0]
    part_rows = rows // 4
    width = q_all.shape[1] - LANES
    group = width // HD
    hidden = jnp.where(kid_ref[...] > qid_ref[...], F32(HIDE), F32(0.0))
    q_all[:, width:] = (q_all[:, width:].astype(F32) + hidden).astype(BF)
    own = OFFSETS.index(0) * part_rows
    contract = (((1,), (1,)), ((), ()))

    for start, stop in spans:
        count = stop - start
        keys, values = kv_ref[start:stop, :HD], kv_ref[start:stop, HD:]
        lane = lax.broadcasted_iota(jnp.int32, (count, LANES), 1)
        block = start // tok + lax.broadcasted_iota(jnp.int32, (count, LANES), 0) // tok
        one_hot = jnp.where(lane == ID_LANE + block, F32(1.0), F32(0.0))
        dk = jnp.zeros((count, HD), F32)
        dv = jnp.zeros((count, HD), F32)
        masked = diagonal and start <= own < stop
        if masked:
            r = lax.broadcasted_iota(jnp.int32, (count, rows), 0)
            c = lax.broadcasted_iota(jnp.int32, (count, rows), 1)
            shift = (own - start) // tok
            future = (r // tok - shift == c // tok) & (r % tok > c % tok) & (c < part_rows)
        for j in range(group):
            mine = (lane >= 3 * j) & (lane < 3 * j + 3)
            pick = jnp.where(mine, F32(1.0), F32(0.0))
            keys_wide = jnp.concatenate([keys, (pick + one_hot).astype(BF)], axis=1)
            values_wide = jnp.concatenate([values, pick.astype(BF)], axis=1)
            at = slice(j * HD, (j + 1) * HD)
            q_j, d_j = q_all[:, at], d_all[:, at]
            q_wide = jnp.concatenate([q_j, q_all[:, width:]], axis=1)
            d_wide = jnp.concatenate([d_j, d_all[:, width:]], axis=1)
            scores = lax.dot_general(keys_wide, q_wide, contract, preferred_element_type=F32)
            grad_probs = lax.dot_general(values_wide, d_wide, contract, preferred_element_type=F32)
            probs = jnp.exp2(scores * F32(SCALE * LOG2E))
            if masked:
                probs = jnp.where(future, F32(0.0), probs)
            grad_scores = (probs * grad_probs).astype(BF)
            dv += jnp.dot(probs.astype(BF), d_j, preferred_element_type=F32)
            dk += jnp.dot(grad_scores, q_j, preferred_element_type=F32)
            dq_acc[at, :] += lax.dot_general(
                keys, grad_scores, (((0,), (0,)), ((), ())), preferred_element_type=F32
            )
        write(start, stop, (dk * F32(SCALE)).astype(BF), dv.astype(BF))


def gather_parts(q_refs, d_parts, q_all, d_all):
    for refs, all_ref in ((q_refs, q_all), (d_parts, d_all)):
        at = 0
        for ref in refs:
            all_ref[at : at + ref.shape[0], :] = ref[...]
            at += ref.shape[0]


def fetch(place_ref, kv_ref, kv_here, sems):
    my_z = place_ref[3]
    rows = kv_ref.shape[1]
    pairs = []
    for n, offset in enumerate(OFFSETS):
        z = lax.rem(my_z + len(OFFSETS) + offset, len(OFFSETS))
        pairs.append((kv_ref.at[z], kv_here.at[pl.ds(n * rows, rows)]))
    return copy_in(pairs, sems)


def cut(start, stop):
    return tuple((at, min(at + CHUNK, stop)) for at in range(start, stop, CHUNK))


def writer(ref, first):
    def write(start, stop, dk, dv):
        ref[start - first : stop - first, :HD] = dk
        ref[start - first : stop - first, HD:] = dv

    return write


def attend_far_kernel(
    tok, place_ref, qid_ref, kid_ref, d0, d1, d2, d3, q0, q1, kv_ref,
    low_ref, high_ref, acc_ref, q_all, d_all, kv_here, sems,
):
    copies = fetch(place_ref, kv_ref, kv_here, sems)
    gather_parts((q0, q1), (d0, d1, d2, d3), q_all, d_all)
    for copy in copies:
        copy.wait()
    acc_ref[...] = jnp.zeros_like(acc_ref)
    edge, end = low_ref.shape[0], kv_here.shape[0]
    args = (place_ref, qid_ref, kid_ref, kv_here)
    rest = (q_all, d_all, acc_ref, tok)
    attend(*args, writer(high_ref, edge), *rest, cut(edge, end), False)
    attend(*args, writer(low_ref, 0), *rest, cut(0, edge), False)


def attend_high_kernel(
    tok, place_ref, qid_ref, kid_ref, d0, d1, d2, d3, q0, q1, acc_in, kv_ref,
    dkv_ref, acc_ref, q_all, d_all, kv_here, sems,
):
    copies = fetch(place_ref, kv_ref, kv_here, sems)
    gather_parts((q0, q1), (d0, d1, d2, d3), q_all, d_all)
    for copy in copies:
        copy.wait()
    acc_ref[...] = acc_in[...]
    end = kv_here.shape[0]
    edge = end - dkv_ref.shape[0]
    attend(
        place_ref, qid_ref, kid_ref, kv_here, writer(dkv_ref, edge), q_all, d_all, acc_ref, tok,
        cut(edge, end), False,
    )


def attend_low_kernel(
    tok, place_ref, qid_ref, kid_ref, d0, d1, d2, d3, q0, q1, acc_in, kv_ref,
    dkv_ref, dq0, dq1, dq2, dq3, q_all, d_all, kv_here, sems, dq_acc,
):
    copies = fetch(place_ref, kv_ref, kv_here, sems)
    gather_parts((q0, q1), (d0, d1, d2, d3), q_all, d_all)
    for copy in copies:
        copy.wait()
    dq_acc[...] = acc_in[...]
    attend(
        place_ref, qid_ref, kid_ref, kv_here, writer(dkv_ref, 0), q_all, d_all, dq_acc, tok,
        cut(0, dkv_ref.shape[0]), True,
    )
    part_rows = dq0.shape[0]
    for j in range(dq_acc.shape[0] // HD):
        at = slice(j * HD, (j + 1) * HD)
        grads = (dq_acc[at, :].T * F32(SCALE)).astype(BF)
        for part, ref in enumerate((dq0, dq1, dq2, dq3)):
            ref[:, at] = grads[part * part_rows : (part + 1) * part_rows]


def join_high_kernel(place_ref, near_ref, far_ref, *out_refs):
    at = 0
    for out_ref in out_refs:
        rows = slice(at, at + out_ref.shape[0])
        out_ref[...] = (near_ref[rows].astype(F32) + far_ref[rows].astype(F32)).astype(BF)
        at += out_ref.shape[0]


def join_low_kernel(place_ref, near_ref, far_ref, ahead_ref, back_ref, *out_refs):
    rows = out_refs[0].shape[0]
    for n, out_ref in enumerate(out_refs):
        at = slice(n * rows, (n + 1) * rows)
        total = near_ref[at].astype(F32) + far_ref[at].astype(F32)
        if n in (1, 2):
            total += ahead_ref[(n - 1) * rows : n * rows].astype(F32)
        if n in (0, 1):
            total += back_ref[n * rows : (n + 1) * rows].astype(F32)
        out_ref[...] = total.astype(BF)


def sum_kernel(place_ref, *refs):
    dq_refs, dkv_refs, out_refs = refs[:4], refs[4:-4], refs[-4:]
    my_head = place_ref[1]
    tok = out_refs[0].shape[0]
    width = dq_refs[0].shape[1]
    for r, out_ref in enumerate(out_refs):
        at = pl.ds(pl.multiple_of(jnp.bitwise_xor(my_head, r) * tok, tok), tok)
        for terms, columns in ((dq_refs, slice(0, width)), (dkv_refs, slice(width, None))):
            total = terms[0][at, :].astype(F32)
            for ref in terms[1:]:
                total += ref[at, :].astype(F32)
            out_ref[:, columns] = total.astype(BF)


def spread_kernel(place_ref, s0, s1, s2, s3, gq_ref, gk_ref, gv_ref):
    my_head = place_ref[1]
    width = s0.shape[1] - 2 * HD
    for r, ref in enumerate((s0, s1, s2, s3)):
        h = jnp.bitwise_xor(my_head, r)
        narrow = pl.ds(pl.multiple_of(h * HD, LANES), HD)
        gq_ref[:, pl.ds(pl.multiple_of(h * width, LANES), width)] = ref[:, :width]
        gk_ref[:, narrow] = ref[:, width : width + HD]
        gv_ref[:, narrow] = ref[:, width + HD :]


def shape_of(*dims, dtype=BF):
    return jax.ShapeDtypeStruct(dims, dtype)


def body(queries, keys, values, outputs, log_norms, grad_output, w_output, block_order):
    tok = grad_output.shape[0]
    heads = lax.axis_size("head")
    inners = lax.axis_size("inner")
    outers = lax.axis_size("outer")
    head, inner, outer = (lax.axis_index(a) for a in ("head", "inner", "outer"))
    zs = inners // 2
    width = queries.shape[1] // heads
    k_width = w_output.shape[1]
    wide = len(WEIGHT_MASKS) * k_width
    part_rows = heads * tok
    rows = outers * part_rows
    my_z = inner % zs
    place = jnp.stack([inner, head, outer, my_z]).astype(jnp.int32)
    smem = pl.BlockSpec(memory_space=pltpu.SMEM)
    vmem = pl.BlockSpec(memory_space=pltpu.VMEM)
    hbm = pl.BlockSpec(memory_space=pltpu.HBM)

    def in_hbm(*arrays):
        return [pltpu.with_memory_space_constraint(x, pltpu.HBM) for x in arrays]

    def swap(x, axis, mask):
        return lax.ppermute(x, axis, xor_route(axis, mask))

    def around(x):
        return [x] + [
            lax.ppermute(x, "outer", [(i, (i + d) % outers) for i in range(outers)])
            for d in range(1, outers)
        ]

    def kernel(fn, shapes, *operands, **options):
        return call(
            fn,
            tuple(shape_of(*dims) for dims in shapes),
            in_specs=[smem] + [vmem] * len(operands),
            out_specs=(vmem,) * len(shapes),
            **options,
        )(place, *operands)

    quarter = width // outers
    sources = (w_output, grad_output, queries, outputs, keys, values, log_norms.T)
    packed = call(
        pack_kernel,
        (shape_of(quarter, k_width),)
        + (shape_of(tok, wide),) * len(TOKEN_MASKS)
        + (shape_of(tok, 2 * width + LANES + 2 * HD),) * heads
        + (shape_of(rows, 1, dtype=F32),)
        + (shape_of(1, LANES, dtype=F32),) * 2,
        in_specs=[smem, smem] + [hbm] * len(sources),
        out_specs=(vmem,) * 12,
        scratch_shapes=[pltpu.VMEM(x.shape, x.dtype) for x in sources[1:]]
        + [pltpu.SemaphoreType.DMA((len(sources),))],
    )(place, block_order, *in_hbm(*sources))
    w_quarter, slots, tokens = packed[0], packed[1:5], packed[5:9]
    qid_col, kid_near, kid_far = packed[9:]
    w_quarters = [swap(w_quarter, "inner", m) for m in WEIGHT_MASKS[1:]]
    slots = [slots[0]] + [swap(x, "inner", m) for x, m in zip(slots[1:], TOKEN_MASKS[1:])]
    tokens = [tokens[0]] + [swap(tokens[r], "head", r) for r in range(1, heads)]
    w_quarters, slots, tokens = lax.optimization_barrier((w_quarters, slots, tokens))

    w_split = around(jnp.stack(w_quarters))
    grads_a = jnp.stack(slots)
    grads_b = swap(grads_a, "head", 2)
    grads_c = swap(grads_a, "head", 1)
    grads_d = swap(grads_b, "head", 1)
    q_part, kv_copies, o_part = call(
        unpack_tokens_kernel,
        (
            shape_of(part_rows, width + LANES),
            pltpu.HBM((zs, part_rows, 2 * HD), BF),
            shape_of(part_rows, width),
        ),
        in_specs=[smem] + [vmem] * heads,
        out_specs=(vmem, hbm, vmem),
        scratch_shapes=[
            pltpu.VMEM((part_rows, 2 * HD), BF),
            pltpu.SemaphoreType.DMA((zs,)),
        ],
    )(place, *tokens)
    planes = [[y * zs + z for z in range(zs)] for y in range(2)]

    def along_z(x, distance):
        route = [(y * zs + z, y * zs + (z + distance) % zs) for y in range(2) for z in range(zs)]
        return lax.ppermute(x, "inner", route)

    kv_near = lax.all_to_all(
        kv_copies, "inner", split_axis=0, concat_axis=0, axis_index_groups=planes, tiled=True
    )
    q_pair = swap(q_part, "outer", 1)
    w_split, grads_a, grads_b, grads_c, grads_d, o_part, q_part, q_pair, kv_near = (
        lax.optimization_barrier(
            (w_split, grads_a, grads_b, grads_c, grads_d, o_part, q_part, q_pair, kv_near)
        )
    )

    partials = call(
        project_kernel,
        (shape_of(heads, tok, width),) * len(TOKEN_MASKS),
        in_specs=[smem] + [hbm] * 9,
        out_specs=(vmem,) * len(TOKEN_MASKS),
        scratch_shapes=[
            pltpu.VMEM((heads, len(TOKEN_MASKS), tok, wide), BF),
            pltpu.VMEM((width, wide), BF),
            pltpu.SemaphoreType.DMA((17,)),
        ],
    )(place, *in_hbm(grads_a, grads_b, grads_c, grads_d, w_output, *w_split))
    partials = list(partials)
    q_part, q_pair, partials[0] = lax.optimization_barrier((q_part, q_pair, partials[0]))
    partials = [partials[0]] + [
        swap(x, "inner", m) for x, m in zip(partials[1:], TOKEN_MASKS[1:])
    ]
    q_pair = jnp.concatenate([q_part, q_pair], 0)
    q_parts = [q_pair, swap(q_pair, "outer", 2)]
    partials, q_parts, o_part = lax.optimization_barrier((partials, q_parts, o_part))

    (d_part,) = kernel(centre_kernel, [(part_rows, width + LANES)], o_part, *partials)
    d_part, kv_near = lax.optimization_barrier((d_part, kv_near))
    d_parts = [d_part] + [swap(d_part, "outer", m) for m in range(1, outers)]
    kv_far = swap(kv_near, "inner", zs)

    low, high = NEXT * part_rows, (zs - NEXT) * part_rows
    acc_shape = shape_of(width, rows, dtype=F32)
    here = [pltpu.VMEM((rows, width + LANES), BF)] * 2
    here += [pltpu.VMEM((zs * part_rows, 2 * HD), BF), pltpu.SemaphoreType.DMA((zs,))]
    (kv_near,) = in_hbm(kv_near)
    far_low, far_high, acc = call(
        functools.partial(attend_far_kernel, tok),
        (shape_of(low, 2 * HD), shape_of(high, 2 * HD), acc_shape),
        in_specs=[smem] + [vmem] * 9,
        out_specs=(vmem,) * 3,
        scratch_shapes=here,
    )(place, qid_col, kid_far, *d_parts, *q_parts, kv_far)
    far_high = swap(far_high, "inner", zs)
    far_low = swap(far_low, "inner", zs)
    near_high, acc = call(
        functools.partial(attend_high_kernel, tok),
        (shape_of(high, 2 * HD), acc_shape),
        in_specs=[smem] + [vmem] * 9 + [hbm],
        out_specs=(vmem,) * 2,
        scratch_shapes=here,
    )(place, qid_col, kid_near, *d_parts, *q_parts, acc, kv_near)
    ahead, back = kernel(join_high_kernel, [(high // 2, 2 * HD)] * 2, near_high, far_high)
    acc, ahead, back = lax.optimization_barrier((acc, ahead, back))
    ahead, back = along_z(ahead, 3), along_z(back, -2)
    near_low, *dq_parts = call(
        functools.partial(attend_low_kernel, tok),
        (shape_of(low, 2 * HD),) + (shape_of(part_rows, width),) * outers,
        in_specs=[smem] + [vmem] * 9 + [hbm],
        out_specs=(vmem,) * (1 + outers),
        scratch_shapes=here + [pltpu.VMEM((width, rows), F32)],
    )(place, qid_col, kid_near, *d_parts, *q_parts, acc, kv_near)

    near_low, far_low, dq_parts, ahead, back = lax.optimization_barrier(
        (near_low, far_low, dq_parts, ahead, back)
    )
    dq_parts = [dq_parts[0]] + [
        swap(dq_parts[m], "outer", m) for m in range(1, outers)
    ]
    parts = kernel(
        join_low_kernel, [(part_rows, 2 * HD)] * NEXT, near_low, far_low, ahead, back
    )
    dkv_parts = [x if n == 0 else along_z(x, n) for x, n in zip(parts, OFFSETS)]
    sums = kernel(sum_kernel, [(tok, width + 2 * HD)] * heads, *dq_parts, *dkv_parts)
    sums = [sums[0]] + [swap(sums[r], "head", r) for r in range(1, heads)]
    return kernel(
        spread_kernel, [(tok, heads * width), (tok, heads * HD), (tok, heads * HD)], *sums
    )


def solution(mesh):
    tokens = P(("head", "inner", "outer"), None)
    in_specs = (tokens,) * 6 + (P("head", "inner"), P())
    return jax.shard_map(
        body, mesh=mesh, in_specs=in_specs, out_specs=(tokens,) * 3, check_vma=False
    )
```

```python
import functools

import jax
import jax.numpy as jnp
from jax import lax
from jax.experimental import pallas as pl
from jax.experimental.pallas import tpu as pltpu
from jax.sharding import PartitionSpec as P

HD = 128
LANES = 128
BF = jnp.bfloat16
F32 = jnp.float32
HIDE = -1e30
SCALE = HD ** (-0.5)
LOG2E = 1.4426950408889634
ID_LANE = 32
CHUNK = 256
VMEM_BYTES = 28 * 1024 * 1024
WEIGHT_MASKS = (0, 2, 4, 6)
TOKEN_MASKS = (0, 1, 8, 9)
OFFSETS = (-1, 0, 1, 2, 3, 4, -3, -2)


def call(kernel, out_shape, **options):
    return pl.pallas_call(
        kernel,
        out_shape=out_shape,
        compiler_params=pltpu.CompilerParams(vmem_limit_bytes=VMEM_BYTES),
        **options,
    )


def xor_route(axis, mask):
    return [(i, i ^ mask) for i in range(lax.axis_size(axis))]


def split_three(x):
    high = x.astype(BF)
    rest = x - high.astype(F32)
    mid = rest.astype(BF)
    low = (rest - mid.astype(F32)).astype(BF)
    return high, mid, low


def pick_three(x, lane_rest):
    high, mid, low = split_three(x)
    zero = jnp.zeros_like(x)
    return (
        jnp.where(lane_rest == 0, high.astype(F32), zero)
        + jnp.where(lane_rest == 1, mid.astype(F32), zero)
        + jnp.where(lane_rest == 2, low.astype(F32), zero)
    ).astype(BF)


def lane_head(shape):
    lane = lax.broadcasted_iota(jnp.int32, shape, len(shape) - 1)
    head = lax.shift_right_logical(lane * 171, 9)
    return lane, head, lane - 3 * head


def ids_kernel(place_ref, order_ref, qid_ref, near_ref, far_ref):
    inner, outer, my_z = place_ref[0], place_ref[2], place_ref[3]
    zs, outers, heads = len(OFFSETS), 4, 4
    inners = 2 * zs
    tok = qid_ref.shape[0] // (outers * heads)
    for d in range(outers):
        o = jnp.bitwise_xor(outer, d)
        for h in range(heads):
            block = order_ref[(h * inners + inner) * outers + o]
            at = (d * heads + h) * tok
            qid_ref[at : at + tok, :] = jnp.full((tok, 1), block, jnp.int32).astype(F32)
    lane = lax.broadcasted_iota(jnp.int32, (1, LANES), 1)
    plane = inner // zs
    for ref, y in ((near_ref, plane), (far_ref, 1 - plane)):
        ids = jnp.full((1, LANES), -1, jnp.int32)
        for n, offset in enumerate(OFFSETS):
            z = lax.rem(my_z + zs + offset, zs)
            for h in range(heads):
                block = order_ref[(h * inners + y * zs + z) * outers + outer]
                ids = jnp.where(lane == ID_LANE + n * heads + h, block, ids)
        ref[...] = ids.astype(F32)


def pack_tokens_kernel(place_ref, q_ref, o_ref, k_ref, v_ref, n_ref, *out_refs):
    my_head = place_ref[1]
    rows = q_ref.shape[0]
    heads = len(out_refs)
    width = q_ref.shape[1] // heads
    group = width // HD
    norms = n_ref[...].astype(F32)
    _, _, lane_rest = lane_head((rows, LANES))
    lane, lane_h, _ = lane_head((heads * group, LANES))
    row = lax.broadcasted_iota(jnp.int32, (heads * group, LANES), 0)
    for r, out_ref in enumerate(out_refs):
        h = jnp.bitwise_xor(my_head, r)
        columns = pl.ds(pl.multiple_of(h * width, LANES), width)
        narrow = pl.ds(pl.multiple_of(h * HD, LANES), HD)
        out_ref[:, :width] = q_ref[:, columns]
        chosen = (row == h * group + lane_h) & (lane_h < group)
        spread = lax.dot_general(
            norms,
            jnp.where(chosen, F32(1.0), F32(0.0)),
            (((0,), (0,)), ((), ())),
            preferred_element_type=F32,
        ) * F32(-(HD**0.5))
        out_ref[:, width : width + LANES] = pick_three(spread, lane_rest)
        at = width + LANES
        out_ref[:, at : at + HD] = k_ref[:, narrow]
        out_ref[:, at + HD : at + 2 * HD] = v_ref[:, narrow]
        out_ref[:, at + 2 * HD :] = o_ref[:, columns]


def unpack_tokens_kernel(place_ref, t0, t1, t2, t3, q_ref, kv_ref, o_ref, kv_here, sems):
    my_head = place_ref[1]
    rows = t0.shape[0]
    q_width, kv_width = q_ref.shape[1], kv_here.shape[1]
    for r, ref in enumerate((t0, t1, t2, t3)):
        h = jnp.bitwise_xor(my_head, r)
        at = pl.ds(pl.multiple_of(h * rows, rows), rows)
        q_ref[at, :] = ref[:, :q_width]
        kv_here[at, :] = ref[:, q_width : q_width + kv_width]
        o_ref[at, :] = ref[:, q_width + kv_width :]
    for copy in copy_in([(kv_here, kv_ref.at[n]) for n in range(kv_ref.shape[0])], sems):
        copy.wait()


def pack_grads_kernel(place_ref, g_ref, *out_refs):
    my_inner = place_ref[0]
    width = out_refs[0].shape[1] // len(WEIGHT_MASKS)
    for m, out_ref in enumerate(out_refs):
        for r, mask in enumerate(WEIGHT_MASKS):
            block = jnp.bitwise_xor(my_inner, TOKEN_MASKS[m] ^ mask)
            start = pl.multiple_of(block * width, LANES)
            out_ref[:, r * width : (r + 1) * width] = g_ref[:, pl.ds(start, width)]


def copy_in(pairs, sems):
    copies = [pltpu.make_async_copy(a, b, sems.at[n]) for n, (a, b) in enumerate(pairs)]
    for copy in copies:
        copy.start()
    return copies


def pack_kernel(
    place_ref, order_ref, w_ref, g_ref, q_ref, o_ref, k_ref, v_ref, n_ref,
    wq_ref, s0, s1, s2, s3, t0, t1, t2, t3, qid_ref, near_ref, far_ref,
    g_here, q_here, o_here, k_here, v_here, n_here, sems,
):
    quarter = wq_ref.shape[0]
    rows = pl.ds(pl.multiple_of(place_ref[2] * quarter, 16), quarter)
    pairs = (
        (w_ref.at[rows], wq_ref), (g_ref, g_here), (q_ref, q_here), (o_ref, o_here),
        (k_ref, k_here), (v_ref, v_here), (n_ref, n_here),
    )
    copies = copy_in(pairs, sems)
    ids_kernel(place_ref, order_ref, qid_ref, near_ref, far_ref)
    for copy in copies:
        copy.wait()
    pack_grads_kernel(place_ref, g_here, s0, s1, s2, s3)
    pack_tokens_kernel(place_ref, q_here, o_here, k_here, v_here, n_here, t0, t1, t2, t3)


def project_kernel(place_ref, ga, gb, gc, gd, w0, x0, x1, x2, x3, *refs):
    out_refs, (g_all, w_all, sems) = refs[:-3], refs[-3:]
    my_head, my_outer = place_ref[1], place_ref[2]
    groups, rows, wide = ga.shape
    width = w0.shape[1]
    count = groups * rows
    quarter = x0.shape[1]
    pairs = [(ref, g_all.at[n]) for n, ref in enumerate((ga, gb, gc, gd))]
    pairs.append((w0, w_all.at[:, pl.ds(0, width)]))
    for d, ref in enumerate((x0, x1, x2, x3)):
        owner = lax.rem(my_outer + 4 - d, 4)
        at = pl.ds(pl.multiple_of(owner * quarter, 16), quarter)
        for j in range(ref.shape[0]):
            pairs.append((ref.at[j], w_all.at[at, pl.ds((1 + j) * width, width)]))
    for copy in copy_in(pairs, sems):
        copy.wait()
    total = lax.dot_general(
        g_all[...].reshape(4 * count, wide), w_all[...], (((1,), (1,)), ((), ())),
        preferred_element_type=F32,
    ).astype(BF)
    for n, mask in enumerate((0, 2, 1, 3)):
        owner = jnp.bitwise_xor(my_head, mask)
        for m, out_ref in enumerate(out_refs):
            at = n * count + m * rows
            out_ref[owner] = total[at : at + rows]


def centre_kernel(place_ref, o_ref, p0, p1, p2, p3, out_ref):
    total = p0[...].astype(F32)
    for p_ref in (p1, p2, p3):
        total += p_ref[...].astype(F32)
    rows, width = o_ref.shape
    grads = total.astype(BF).reshape(rows, width)
    out_ref[:, :width] = grads
    product = grads.astype(F32) * o_ref[...].astype(F32)
    _, lane_h, lane_rest = lane_head((rows, LANES))
    spread = jnp.zeros((rows, LANES), F32)
    for j in range(width // HD):
        delta = jnp.sum(product[:, j * HD : (j + 1) * HD], axis=1, keepdims=True)
        spread = jnp.where(lane_h == j, -delta, spread)
    out_ref[:, width:] = pick_three(spread, lane_rest)


def chunk_rows(step):
    return pl.ds(pl.multiple_of(step * CHUNK, CHUNK), CHUNK)


def score_probs(qid_ref, kid_ref, kv_ref, q_all, tok, step, diagonal, use):
    rows = q_all.shape[0]
    part_rows = rows // 4
    width = q_all.shape[1] - LANES
    hidden = jnp.where(kid_ref[...] > qid_ref[...], F32(HIDE), F32(0.0))
    q_extra = (q_all[:, width:].astype(F32) + hidden).astype(BF)
    own = OFFSETS.index(0) * part_rows
    count = CHUNK
    keys = kv_ref[chunk_rows(step), :HD]
    lane = lax.broadcasted_iota(jnp.int32, (count, LANES), 1)
    block = step * (CHUNK // tok) + lax.broadcasted_iota(jnp.int32, (count, LANES), 0) // tok
    one_hot = jnp.where(lane == ID_LANE + block, F32(1.0), F32(0.0))
    if diagonal:
        r = lax.broadcasted_iota(jnp.int32, (count, rows), 0)
        c = lax.broadcasted_iota(jnp.int32, (count, rows), 1)
        shift = (own - step * CHUNK) // tok
        future = (r // tok - shift == c // tok) & (r % tok > c % tok) & (c < part_rows)
    for j in range(width // HD):
        mine = (lane >= 3 * j) & (lane < 3 * j + 3)
        pick = jnp.where(mine, F32(1.0), F32(0.0))
        keys_wide = jnp.concatenate([keys, (pick + one_hot).astype(BF)], axis=1)
        q_wide = jnp.concatenate([q_all[:, j * HD : (j + 1) * HD], q_extra], axis=1)
        scores = lax.dot_general(
            keys_wide, q_wide, (((1,), (1,)), ((), ())), preferred_element_type=F32
        )
        probs = jnp.exp2(scores * F32(SCALE * LOG2E))
        if diagonal:
            probs = jnp.where(future, F32(0.0), probs)
        use(j, probs)


def gradients(kv_ref, dkv_ref, q_all, d_all, dq_acc, step, each_probs):
    count = CHUNK
    width = q_all.shape[1] - LANES
    at_rows = chunk_rows(step)
    keys, values = kv_ref[at_rows, :HD], kv_ref[at_rows, HD:]
    lane = lax.broadcasted_iota(jnp.int32, (count, LANES), 1)
    sums = [jnp.zeros((count, HD), F32), jnp.zeros((count, HD), F32)]

    def use(j, probs):
        mine = (lane >= 3 * j) & (lane < 3 * j + 3)
        pick = jnp.where(mine, F32(1.0), F32(0.0))
        values_wide = jnp.concatenate([values, pick.astype(BF)], axis=1)
        at = slice(j * HD, (j + 1) * HD)
        q_j, d_j = q_all[:, at], d_all[:, at]
        d_wide = jnp.concatenate([d_j, d_all[:, width:]], axis=1)
        grad_probs = lax.dot_general(
            values_wide, d_wide, (((1,), (1,)), ((), ())), preferred_element_type=F32
        )
        grad_scores = (probs.astype(F32) * grad_probs).astype(BF)
        sums[1] += jnp.dot(probs.astype(BF), d_j, preferred_element_type=F32)
        sums[0] += jnp.dot(grad_scores, q_j, preferred_element_type=F32)
        dq_acc[:, at] += lax.dot_general(
            grad_scores, keys, (((0,), (0,)), ((), ())), preferred_element_type=F32
        )

    each_probs(use)
    dkv_ref[at_rows, :HD] = (sums[0] * F32(SCALE)).astype(BF)
    dkv_ref[at_rows, HD:] = sums[1].astype(BF)


def gather_parts(refs, all_ref):
    at = 0
    for ref in refs:
        all_ref[at : at + ref.shape[0], :] = ref[...]
        at += ref.shape[0]


def fetch(place_ref, kv_ref, kv_here, sems):
    my_z = place_ref[3]
    rows = kv_ref.shape[1]
    pairs = []
    for n, offset in enumerate(OFFSETS):
        z = lax.rem(my_z + len(OFFSETS) + offset, len(OFFSETS))
        pairs.append((kv_ref.at[z], kv_here.at[pl.ds(n * rows, rows)]))
    return copy_in(pairs, sems)


def near_probs_kernel(
    tok, place_ref, qid_ref, kid_ref, q0, q1, kv_ref, probs_ref, q_all, kv_here, sems
):
    copies = fetch(place_ref, kv_ref, kv_here, sems)
    gather_parts((q0, q1), q_all)
    for copy in copies:
        copy.wait()

    @pl.loop(0, kv_here.shape[0] // CHUNK)
    def _(step):
        def store(j, probs):
            probs_ref[j, chunk_rows(step), :] = probs.astype(BF)

        score_probs(qid_ref, kid_ref, kv_here, q_all, tok, step, True, store)


def attend_far_kernel(
    tok, place_ref, qid_ref, kid_ref, d0, d1, d2, d3, q0, q1, kv_ref,
    dkv_ref, acc_ref, q_all, d_all, kv_here, sems,
):
    copies = fetch(place_ref, kv_ref, kv_here, sems)
    gather_parts((q0, q1), q_all)
    gather_parts((d0, d1, d2, d3), d_all)
    for copy in copies:
        copy.wait()
    acc_ref[...] = jnp.zeros_like(acc_ref)

    @pl.loop(0, dkv_ref.shape[0] // CHUNK)
    def _(step):
        each = functools.partial(
            score_probs, qid_ref, kid_ref, kv_here, q_all, tok, step, False
        )
        gradients(kv_here, dkv_ref, q_all, d_all, acc_ref, step, each)


def attend_near_kernel(
    place_ref, d0, d1, d2, d3, q0, q1, acc_in, probs_ref, kv_ref,
    dkv_ref, dq0, dq1, dq2, dq3, q_all, d_all, kv_here, sems, dq_acc,
):
    copies = fetch(place_ref, kv_ref, kv_here, sems)
    gather_parts((q0, q1), q_all)
    gather_parts((d0, d1, d2, d3), d_all)
    for copy in copies:
        copy.wait()
    dq_acc[...] = acc_in[...]

    @pl.loop(0, dkv_ref.shape[0] // CHUNK)
    def _(step):
        def each(use):
            for j in range(probs_ref.shape[0]):
                use(j, probs_ref[j, chunk_rows(step), :])

        gradients(kv_here, dkv_ref, q_all, d_all, dq_acc, step, each)

    part_rows = dq0.shape[0]
    for part, ref in enumerate((dq0, dq1, dq2, dq3)):
        grads = dq_acc[part * part_rows : (part + 1) * part_rows, :]
        ref[...] = (grads * F32(SCALE)).astype(BF)


def join_kernel(place_ref, near_ref, far_ref, out_ref, here, sems):
    my_z = place_ref[3]
    zs, rows = out_ref.shape[:2]
    here[...] = (near_ref[...].astype(F32) + far_ref[...].astype(F32)).astype(BF)
    pairs = []
    for n, offset in enumerate(OFFSETS):
        z = lax.rem(my_z + zs + offset, zs)
        pairs.append((here.at[pl.ds(n * rows, rows)], out_ref.at[z]))
    for copy in copy_in(pairs, sems):
        copy.wait()


def sum_kernel(place_ref, *refs):
    dq_refs, dkv_ref, out_refs = refs[:4], refs[4], refs[-4:]
    dkv_refs = [dkv_ref.at[z] for z in range(dkv_ref.shape[0])]
    my_head = place_ref[1]
    tok = out_refs[0].shape[0]
    width = dq_refs[0].shape[1]
    for r, out_ref in enumerate(out_refs):
        at = pl.ds(pl.multiple_of(jnp.bitwise_xor(my_head, r) * tok, tok), tok)
        for terms, columns in ((dq_refs, slice(0, width)), (dkv_refs, slice(width, None))):
            total = terms[0][at, :].astype(F32)
            for ref in terms[1:]:
                total += ref[at, :].astype(F32)
            out_ref[:, columns] = total.astype(BF)


def spread_kernel(place_ref, s0, s1, s2, s3, gq_ref, gk_ref, gv_ref):
    my_head = place_ref[1]
    width = s0.shape[1] - 2 * HD
    for r, ref in enumerate((s0, s1, s2, s3)):
        h = jnp.bitwise_xor(my_head, r)
        narrow = pl.ds(pl.multiple_of(h * HD, LANES), HD)
        gq_ref[:, pl.ds(pl.multiple_of(h * width, LANES), width)] = ref[:, :width]
        gk_ref[:, narrow] = ref[:, width : width + HD]
        gv_ref[:, narrow] = ref[:, width + HD :]


def shape_of(*dims, dtype=BF):
    return jax.ShapeDtypeStruct(dims, dtype)


def body(queries, keys, values, outputs, log_norms, grad_output, w_output, block_order):
    tok = grad_output.shape[0]
    heads = lax.axis_size("head")
    inners = lax.axis_size("inner")
    outers = lax.axis_size("outer")
    head, inner, outer = (lax.axis_index(a) for a in ("head", "inner", "outer"))
    zs = inners // 2
    width = queries.shape[1] // heads
    k_width = w_output.shape[1]
    wide = len(WEIGHT_MASKS) * k_width
    part_rows = heads * tok
    rows = outers * part_rows
    my_z = inner % zs
    place = jnp.stack([inner, head, outer, my_z]).astype(jnp.int32)
    smem = pl.BlockSpec(memory_space=pltpu.SMEM)
    vmem = pl.BlockSpec(memory_space=pltpu.VMEM)
    hbm = pl.BlockSpec(memory_space=pltpu.HBM)

    def in_hbm(*arrays):
        return [pltpu.with_memory_space_constraint(x, pltpu.HBM) for x in arrays]

    def swap(x, axis, mask):
        return lax.ppermute(x, axis, xor_route(axis, mask))

    def around(x):
        return [x] + [
            lax.ppermute(x, "outer", [(i, (i + d) % outers) for i in range(outers)])
            for d in range(1, outers)
        ]

    def kernel(fn, shapes, *operands, **options):
        return call(
            fn,
            tuple(shape_of(*dims) for dims in shapes),
            in_specs=[smem] + [vmem] * len(operands),
            out_specs=(vmem,) * len(shapes),
            **options,
        )(place, *operands)

    quarter = width // outers
    sources = (w_output, grad_output, queries, outputs, keys, values, log_norms.T)
    packed = call(
        pack_kernel,
        (shape_of(quarter, k_width),)
        + (shape_of(tok, wide),) * len(TOKEN_MASKS)
        + (shape_of(tok, 2 * width + LANES + 2 * HD),) * heads
        + (shape_of(rows, 1, dtype=F32),)
        + (shape_of(1, LANES, dtype=F32),) * 2,
        in_specs=[smem, smem] + [hbm] * len(sources),
        out_specs=(vmem,) * 12,
        scratch_shapes=[pltpu.VMEM(x.shape, x.dtype) for x in sources[1:]]
        + [pltpu.SemaphoreType.DMA((len(sources),))],
    )(place, block_order, *in_hbm(*sources))
    w_quarter, slots, tokens = packed[0], packed[1:5], packed[5:9]
    qid_col, kid_near, kid_far = packed[9:]
    tokens = [tokens[0]] + [swap(tokens[r], "head", r) for r in range(1, heads)]
    slots, tokens[1] = lax.optimization_barrier((slots, tokens[1]))
    slots = [slots[0]] + [swap(x, "inner", m) for x, m in zip(slots[1:], TOKEN_MASKS[1:])]
    w_quarters = [swap(w_quarter, "inner", m) for m in WEIGHT_MASKS[1:]]
    w_quarters, slots, tokens = lax.optimization_barrier((w_quarters, slots, tokens))

    w_split = around(jnp.stack(w_quarters))
    grads_a = jnp.stack(slots)
    grads_b = swap(grads_a, "head", 2)
    grads_c = swap(grads_a, "head", 1)
    grads_d = swap(grads_b, "head", 1)
    w_split[1], tokens = lax.optimization_barrier((w_split[1], tokens))
    q_part, kv_copies, o_part = call(
        unpack_tokens_kernel,
        (
            shape_of(part_rows, width + LANES),
            pltpu.HBM((zs, part_rows, 2 * HD), BF),
            shape_of(part_rows, width),
        ),
        in_specs=[smem] + [vmem] * heads,
        out_specs=(vmem, hbm, vmem),
        scratch_shapes=[
            pltpu.VMEM((part_rows, 2 * HD), BF),
            pltpu.SemaphoreType.DMA((zs,)),
        ],
    )(place, *tokens)
    planes = [[y * zs + z for z in range(zs)] for y in range(2)]

    def along_z(x, distance):
        route = [(y * zs + z, y * zs + (z + distance) % zs) for y in range(2) for z in range(zs)]
        return lax.ppermute(x, "inner", route)

    kv_near = lax.all_to_all(
        kv_copies, "inner", split_axis=0, concat_axis=0, axis_index_groups=planes, tiled=True
    )
    q_pair = swap(q_part, "outer", 1)
    w_split, grads_a, grads_b, grads_c, grads_d, o_part, q_part, q_pair = (
        lax.optimization_barrier(
            (w_split, grads_a, grads_b, grads_c, grads_d, o_part, q_part, q_pair)
        )
    )

    partials = call(
        project_kernel,
        (shape_of(heads, tok, width),) * len(TOKEN_MASKS),
        in_specs=[smem] + [pl.BlockSpec(memory_space=pl.ANY)] * 9,
        out_specs=(vmem,) * len(TOKEN_MASKS),
        scratch_shapes=[
            pltpu.VMEM((heads, len(TOKEN_MASKS), tok, wide), BF),
            pltpu.VMEM((width, wide), BF),
            pltpu.SemaphoreType.DMA((17,)),
        ],
    )(place, grads_a, grads_b, grads_c, grads_d, w_output, *w_split)
    partials = list(partials)
    q_part, q_pair, partials[0] = lax.optimization_barrier((q_part, q_pair, partials[0]))
    partials = [partials[0]] + [
        swap(x, "inner", m) for x, m in zip(partials[1:], TOKEN_MASKS[1:])
    ]
    q_pair = jnp.concatenate([q_part, q_pair], 0)
    q_parts = [q_pair, swap(q_pair, "outer", 2)]
    partials, q_parts, o_part = lax.optimization_barrier((partials, q_parts, o_part))

    (d_part,) = kernel(centre_kernel, [(part_rows, width + LANES)], o_part, *partials)
    d_part, kv_near = lax.optimization_barrier((d_part, kv_near))
    d_parts = [d_part] + [swap(d_part, "outer", m) for m in range(1, outers)]
    kv_near, d_part = lax.optimization_barrier((kv_near, d_part))
    kv_far = swap(kv_near, "inner", zs)

    kv_rows = zs * part_rows
    acc_shape = shape_of(rows, width, dtype=F32)
    here = [pltpu.VMEM((rows, width + LANES), BF)] * 2
    here += [pltpu.VMEM((kv_rows, 2 * HD), BF), pltpu.SemaphoreType.DMA((zs,))]
    (kv_near,) = in_hbm(kv_near)
    near_probs = call(
        functools.partial(near_probs_kernel, tok),
        shape_of(width // HD, kv_rows, rows),
        in_specs=[smem] + [vmem] * 4 + [hbm],
        out_specs=vmem,
        scratch_shapes=[here[0]] + here[2:],
    )(place, qid_col, kid_near, *q_parts, kv_near)
    d_parts, near_probs = lax.optimization_barrier((d_parts, near_probs))
    dkv_far, acc = call(
        functools.partial(attend_far_kernel, tok),
        (shape_of(kv_rows, 2 * HD), acc_shape),
        in_specs=[smem] + [vmem] * 9,
        out_specs=(vmem,) * 2,
        scratch_shapes=here,
    )(place, qid_col, kid_far, *d_parts, *q_parts, kv_far)
    dkv_far = swap(dkv_far, "inner", zs)
    dkv_near, *dq_parts = call(
        attend_near_kernel,
        (shape_of(kv_rows, 2 * HD),) + (shape_of(part_rows, width),) * outers,
        in_specs=[smem] + [vmem] * 8 + [hbm],
        out_specs=(vmem,) * (1 + outers),
        scratch_shapes=here + [pltpu.VMEM((rows, width), F32)],
    )(place, *d_parts, *q_parts, acc, near_probs, kv_near)

    dkv_near, dkv_far, dq_parts = lax.optimization_barrier((dkv_near, dkv_far, dq_parts))
    dq_parts = [dq_parts[0]] + [
        swap(dq_parts[m], "outer", m) for m in range(1, outers)
    ]
    dkv = call(
        join_kernel,
        pltpu.HBM((zs, part_rows, 2 * HD), BF),
        in_specs=[smem] + [vmem] * 2,
        out_specs=hbm,
        scratch_shapes=[pltpu.VMEM((kv_rows, 2 * HD), BF), pltpu.SemaphoreType.DMA((zs,))],
    )(place, dkv_near, dkv_far)
    dkv = lax.all_to_all(
        dkv, "inner", split_axis=0, concat_axis=0, axis_index_groups=planes, tiled=True
    )
    sums = kernel(sum_kernel, [(tok, width + 2 * HD)] * heads, *dq_parts, dkv)
    sums = [sums[0]] + [swap(sums[r], "head", r) for r in range(1, heads)]
    return kernel(
        spread_kernel, [(tok, heads * width), (tok, heads * HD), (tok, heads * HD)], *sums
    )


def solution(mesh):
    tokens = P(("head", "inner", "outer"), None)
    in_specs = (tokens,) * 6 + (P("head", "inner"), P())
    return jax.shard_map(
        body, mesh=mesh, in_specs=in_specs, out_specs=(tokens,) * 3, check_vma=False
    )
```
